512 devices in a mesh: row: 16 (over y, core), col: 32 (over x, z).
Axes of the slice: x: 4, y: 8, z: 8, core: 2. Of those that a mesh axis runs over, the one named last changes fastest.
Arguments:
- tokens: bfloat16 [256, 12288], P('col', 'row'), may hold values from -6 to 6
- w_in: bfloat16 [12288, 24576], P('row', 'col'), may hold values from -0.0546875 to 0.0546875
- w_out: bfloat16 [24576, 12288], P('col', 'row'), may hold values from -0.0390625 to 0.0390625
- grad_out: bfloat16 [256, 12288], P('col', 'row'), may hold values from -6 to 6
Outputs:
- output: bfloat16 [256, 12288], P('col', 'row')
- grad_tokens: bfloat16 [256, 12288], P('col', 'row')
- grad_w_in: bfloat16 [12288, 24576], P('row', 'col')
- grad_w_out: bfloat16 [24576, 12288], P('col', 'row')
The draws below stay inside these ranges and needn't reach their ends.
All inputs are finite; a program needn't handle non-finite values.
Results may differ from the reference program's by a relative error of at most 0.005.
Values may be sent and summed in bfloat16 or wider, within the bound.
A program may use at most 64 MiB of HBM per device.

```python
import math
import jax
import jax.numpy as jnp
from jax import lax

D = 12288
FF = 24576
TOKENS = 256


def levels(own_key, shape, cuts, smallest, high):
    def one(dim, parts):
        heights = jax.random.uniform(jax.random.fold_in(jax.random.fold_in(own_key, 6), dim), (parts,), jnp.float32, smallest / len(cuts), high / len(cuts))
        return jnp.repeat(jnp.exp(heights), shape[dim] // parts).reshape((-1,) + (1,) * (len(shape) - dim - 1))

    gain = one(*cuts[0])
    for cut in cuts[1:]:
        gain = gain * one(*cut)
    return gain


def normal_values(stream_key, extent, width, bound, pieces=(), dtype=jnp.bfloat16):
    result = width * jax.random.normal(stream_key, extent, jnp.float32)
    if pieces:
        result = result * levels(stream_key, extent, pieces, -0.22, 0.18)
    return jnp.clip(result, -bound, bound).astype(dtype)


def setup_inputs(seed: int = 0) -> dict:
    key_of = jax.random.split(jax.random.key(seed), 5)
    return {
        "tokens": normal_values(key_of[0], (TOKENS, D), 1.0, 6.0, ((0, 32), (1, 16))),
        "w_in": normal_values(key_of[1], (D, FF), D ** -0.5, 0.0546875, ((0, 16), (1, 32))),
        "w_out": normal_values(key_of[2], (FF, D), FF ** -0.5, 0.0390625, ((0, 32), (1, 16))),
        "grad_out": normal_values(key_of[3], (TOKENS, D), 1.0, 6.0, ((0, 32), (1, 16))),
    }


gelu_scale = math.sqrt(2.0 / math.pi)

def gelu_parts(hidden):
    inner = gelu_scale * (hidden + 0.044715 * hidden * hidden * hidden)
    tanh_value = jnp.tanh(inner)
    act_value = 0.5 * hidden * (1.0 + tanh_value)
    act_slope = 0.5 * (1.0 + tanh_value) + 0.5 * hidden * (1.0 - tanh_value * tanh_value) * gelu_scale * (1.0 + 3.0 * 0.044715 * hidden * hidden)
    return (act_value, act_slope)

def reference(tokens, w_in, w_out, grad_out):
    hidden = jnp.dot(tokens, w_in, preferred_element_type=jnp.float32)
    act_value, act_slope = gelu_parts(hidden)
    act = act_value.astype(jnp.bfloat16)
    output = jnp.dot(act, w_out, preferred_element_type=jnp.float32).astype(jnp.bfloat16)
    grad_w_out = lax.dot_general(act, grad_out, (((0,), (0,)), ((), ())), preferred_element_type=jnp.float32).astype(jnp.bfloat16)
    grad_act = lax.dot_general(grad_out, w_out, (((1,), (1,)), ((), ())), preferred_element_type=jnp.float32)
    grad_hidden = (grad_act * act_slope).astype(jnp.bfloat16)
    grad_w_in = lax.dot_general(tokens, grad_hidden, (((0,), (0,)), ((), ())), preferred_element_type=jnp.float32).astype(jnp.bfloat16)
    grad_tokens = lax.dot_general(grad_hidden, w_in, (((1,), (1,)), ((), ())), preferred_element_type=jnp.float32).astype(jnp.bfloat16)
    return (output, grad_tokens, grad_w_in, grad_w_out)
```

```python
import functools
import math

import jax
import jax.numpy as jnp
from jax import lax
from jax.experimental import pallas as pl
from jax.experimental.pallas import tpu as pltpu
from jax.sharding import PartitionSpec as P

gelu_scale = math.sqrt(2.0 / math.pi)
MESH = pl.DeviceIdType.MESH
F32 = jnp.float32
BF16 = jnp.bfloat16

NX = 4
OFFSETS = (0, 1, 3, 2)
BACK = (0, 2, 1, 3)
GROUPS = ((0,), (1, 2), (3,))


def gelu_parts(hidden):
    inner = gelu_scale * (hidden + 0.044715 * hidden * hidden * hidden)
    tanh_value = jnp.tanh(inner)
    act_value = 0.5 * hidden * (1.0 + tanh_value)
    act_slope = 0.5 * (1.0 + tanh_value) + 0.5 * hidden * (
        1.0 - tanh_value * tanh_value
    ) * gelu_scale * (1.0 + 3.0 * 0.044715 * hidden * hidden)
    return (act_value, act_slope)


def mm(left, right):
    return jnp.dot(left, right, preferred_element_type=F32)


def far_first(n):
    return sorted(range(1, n), key=lambda k: (-min(k, n - k), k))


def scratch_list(ny, nz, width, hid):
    half, chunk = hid // 2, nz * 8
    s = {
        "win": pltpu.VMEM((width, hid), BF16),
        "wout": pltpu.VMEM((hid, width), BF16),
        "win_t": pltpu.VMEM((hid, width), BF16),
        "wout_t": pltpu.VMEM((width, hid), BF16),
        "act_t": pltpu.VMEM((hid, NX * chunk), BF16),
        "tok_t": pltpu.VMEM((width, NX * chunk), BF16),
        "comb": pltpu.VMEM((nz, 16, width), BF16),
        "tg": pltpu.VMEM((NX, 2, chunk, width), BF16),
        "actb": pltpu.VMEM((NX, chunk, hid), BF16),
        "ghb": pltpu.VMEM((NX, chunk, hid), BF16),
        "ds": pltpu.VMEM((NX, 2, chunk, width), BF16),
        "dr": pltpu.VMEM((NX, 2, chunk, width), BF16),
        "down": pltpu.VMEM((2, chunk, width), F32),
        "zs": pltpu.VMEM((nz, 16, width), BF16),
        "zr": pltpu.VMEM((nz, 16, width), BF16),
    }
    for g, slots in enumerate(GROUPS):
        n = len(slots)
        s[f"hk{g}"] = pltpu.VMEM((2, n * chunk, half), F32)
        s[f"xs{g}"] = pltpu.VMEM((2, n * chunk, half), F32)
        s[f"xr{g}"] = pltpu.VMEM((2, n * chunk, half), F32)
        s[f"bs{g}"] = pltpu.VMEM((ny, n * 16, half), BF16)
        s[f"br{g}"] = pltpu.VMEM((ny, n * 16, half), BF16)
        s[f"cb{g}"] = pltpu.VMEM((2, ny, n * 16, half), BF16)
    dma = pltpu.SemaphoreType.DMA
    ng = len(GROUPS)
    s["w_sem"] = dma((4,))
    for name, shape in (
        ("az", (nz,)),
        ("ax", (NX,)),
        ("cx", (ng,)),
        ("by", (ng, ny)),
        ("cy", (ng, ny)),
        ("cf", (ng,)),
        ("dx", (NX,)),
        ("dz", (nz,)),
    ):
        s[name + "_s"] = dma(shape)
        s[name + "_r"] = dma(shape)
    return s


def kernel(ny, nz, names, tok_ref, grad_ref, win_hbm, wout_hbm, out_ref, gt_ref, gwin_ref, gwout_ref, *scratch):
    r = dict(zip(names, scratch))
    width, hid = r["win"].shape
    half, chunk = hid // 2, nz * 8
    row, col = lax.axis_index("row"), lax.axis_index("col")
    y, core = row // 2, lax.rem(row, 2)
    x, z = col // nz, lax.rem(col, nz)
    sibling = {"row": y * 2 + (1 - core), "col": col}

    def at_y(k):
        return {"row": lax.rem(y + k, ny) * 2 + core, "col": col}

    def at_x(k):
        return {"row": row, "col": lax.rem(x + k, NX) * nz + z}

    def at_z(k):
        return {"row": row, "col": x * nz + lax.rem(z + k, nz)}

    sent = []

    def send(src, dst, sem, send_at, recv_at, device):
        copy = pltpu.make_async_remote_copy(
            src_ref=src,
            dst_ref=dst,
            send_sem=r[sem + "_s"].at[send_at],
            recv_sem=r[sem + "_r"].at[recv_at],
            device_id=device,
            device_id_type=MESH,
        )
        copy.start()
        sent.append(copy)
        return copy

    weight_copies = []
    for h in range(2):
        start = pl.multiple_of((core if h == 0 else 1 - core) * half, half)
        weight_copies.append(
            pltpu.make_async_copy(
                win_hbm.at[:, pl.ds(start, half)], r["win"].at[:, pl.ds(h * half, half)], r["w_sem"].at[h]
            )
        )
        weight_copies.append(
            pltpu.make_async_copy(
                wout_hbm.at[pl.ds(start, half), :], r["wout"].at[pl.ds(h * half, half), :], r["w_sem"].at[2 + h]
            )
        )
    for copy in weight_copies:
        copy.start()

    barrier = pltpu.get_barrier_semaphore()
    partners = (
        [at_z(k) for k in range(1, nz)]
        + [at_x(k) for k in range(1, NX)]
        + [at_y(k) for k in range(1, ny)]
        + [sibling]
    )
    for device in partners:
        pl.semaphore_signal(barrier, inc=1, device_id=device, device_id_type=MESH)
    r["comb"][z] = jnp.concatenate(
        [tok_ref[...].astype(F32), grad_ref[...].astype(F32)], axis=0
    ).astype(BF16)
    pl.semaphore_wait(barrier, len(partners))

    az = [
        send(r["comb"].at[z], r["comb"].at[z], "az", k, nz - k, at_z(k)) for k in far_first(nz)
    ]
    for copy in weight_copies:
        copy.wait()
    r["wout_t"][...] = r["wout"][...].T
    r["win_t"][...] = r["win"][...].T
    for copy in az:
        copy.wait_recv()
    block = r["comb"][...].astype(F32)
    r["tg"][0, 0] = block[:, :8, :].reshape(chunk, width).astype(BF16)
    r["tg"][0, 1] = block[:, 8:, :].reshape(chunk, width).astype(BF16)

    ax = {}
    for s in (1, 2, 3):
        ax[BACK[s]] = send(r["tg"].at[0], r["tg"].at[BACK[s]], "ax", s, BACK[s], at_x(OFFSETS[s]))

    live = {}

    def rows_of(name, part, slots):
        return jnp.concatenate([r[name][s, part] for s in slots], axis=0)

    def first_products(g):
        slots = GROUPS[g]
        for s in slots:
            if s:
                ax[s].wait_recv()
        hidden = mm(rows_of("tg", 0, slots), r["win"][...])
        grad_act = mm(rows_of("tg", 1, slots), r["wout_t"][...])
        for i, value in enumerate((hidden, grad_act)):
            r[f"xs{g}"][i] = value[:, half:]
            r[f"hk{g}"][i] = value[:, :half]
        live["cx", g] = send(r[f"xs{g}"], r[f"xr{g}"], "cx", g, g, sibling)

    def terms_over_y(g):
        n = len(GROUPS[g])
        live["cx", g].wait_recv()
        both = [r[f"hk{g}"][i] + r[f"xr{g}"][i] for i in range(2)]
        for d in range(ny):
            parts = []
            for i in range(n):
                for j in range(2):
                    at = i * chunk + d * 8
                    parts.append(both[j][at : at + 8])
            r[f"bs{g}"][d] = jnp.concatenate(parts, axis=0).astype(BF16)
        live["by", g] = [
            send(r[f"bs{g}"].at[lax.rem(y + k, ny)], r[f"br{g}"].at[ny - k], "by", (g, k), (g, ny - k), at_y(k))
            for k in far_first(ny)
        ]

    def activate(g):
        n = len(GROUPS[g])
        total = r[f"bs{g}"][y].astype(F32)
        for copy in live["by", g]:
            copy.wait_recv()
        for k in range(1, ny):
            total = total + r[f"br{g}"][k].astype(F32)
        total = total.reshape(n, 2, 8, half)
        act_value, act_slope = gelu_parts(total[:, 0])
        grad_hidden = total[:, 1] * act_slope
        both = jnp.stack([act_value, grad_hidden], axis=1).reshape(n * 16, half)
        r[f"cb{g}"][0, y] = both.astype(BF16)
        own = r[f"cb{g}"].at[0, y]
        live["cy", g] = [
            send(own, own, "cy", (g, k), (g, ny - k), at_y(k)) for k in far_first(ny)
        ]

    def forward(g):
        for copy in live["cy", g]:
            copy.wait_recv()
        live["cf", g] = send(r[f"cb{g}"].at[0], r[f"cb{g}"].at[1], "cf", g, g, sibling)

    def second_products(g):
        slots = GROUPS[g]
        n = len(slots)
        live["cf", g].wait_recv()
        for h in range(2):
            got = r[f"cb{g}"][h].astype(F32).reshape(ny, n, 2, 8, half)
            for i, s in enumerate(slots):
                r["actb"][s, :, h * half : (h + 1) * half] = got[:, i, 0].reshape(chunk, half).astype(BF16)
                r["ghb"][s, :, h * half : (h + 1) * half] = got[:, i, 1].reshape(chunk, half).astype(BF16)
        first, last = slots[0], slots[-1] + 1
        act = r["actb"][first:last].reshape(n * chunk, hid)
        grad_hidden = r["ghb"][first:last].reshape(n * chunk, hid)
        for j, value in enumerate((mm(act, r["wout"][...]), mm(grad_hidden, r["win_t"][...]))):
            for i, s in enumerate(slots):
                part = value[i * chunk : (i + 1) * chunk]
                if s:
                    r["ds"][s, j] = part.astype(BF16)
                else:
                    r["down"][j] = part
        for s in slots:
            if s:
                live["dx", BACK[s]] = send(
                    r["ds"].at[s], r["dr"].at[BACK[s]], "dx", s, BACK[s], at_x(OFFSETS[s])
                )

    first_products(0)
    terms_over_y(0)
    activate(0)
    first_products(1)
    forward(0)
    terms_over_y(1)
    second_products(0)
    first_products(2)
    activate(1)
    terms_over_y(2)
    forward(1)
    activate(2)
    second_products(1)
    forward(2)
    second_products(2)

    tile = min(256, half)
    tokens_all = rows_of("tg", 0, range(NX))
    grad_all = rows_of("tg", 1, range(NX))
    r["act_t"][...] = r["actb"][...].reshape(NX * chunk, hid).T
    r["tok_t"][...] = tokens_all.T
    grad_hidden_all = r["ghb"][...].reshape(NX * chunk, hid)
    for h in range(2):
        start = pl.multiple_of((core if h == 0 else 1 - core) * half, half)
        gwout_ref[pl.ds(start, half), :] = mm(
            r["act_t"][h * half : (h + 1) * half, :], grad_all
        ).astype(BF16)
        gwin_ref[:, pl.ds(start, half)] = mm(
            r["tok_t"][...], grad_hidden_all[:, h * half : (h + 1) * half]
        ).astype(BF16)

    for s in (1, 2, 3):
        live["dx", s].wait_recv()
    sums = []
    for j in range(2):
        value = r["down"][j]
        for s in (1, 2, 3):
            value = value + r["dr"][s, j].astype(F32)
        sums.append(value)
    for d in range(nz):
        r["zs"][d] = jnp.concatenate([v[d * 8 : d * 8 + 8] for v in sums], axis=0).astype(BF16)
    dz = [
        send(r["zs"].at[lax.rem(z + k, nz)], r["zr"].at[nz - k], "dz", k, nz - k, at_z(k)) for k in far_first(nz)
    ]
    total = r["zs"][z].astype(F32)
    for copy in dz:
        copy.wait_recv()
    for k in range(1, nz):
        total = total + r["zr"][k].astype(F32)
    out_ref[...] = total[:8].astype(BF16)
    gt_ref[...] = total[8:].astype(BF16)
    for copy in sent:
        copy.wait_send()


def local(ny, nz, tokens, w_in, w_out, grad_out):
    width, hid = w_in.shape
    scratch = scratch_list(ny, nz, width, hid)
    vmem = pl.BlockSpec(memory_space=pltpu.VMEM)
    any_space = pl.BlockSpec(memory_space=pl.ANY)
    return pl.pallas_call(
        functools.partial(kernel, ny, nz, tuple(scratch)),
        out_shape=(
            jax.ShapeDtypeStruct((8, width), BF16),
            jax.ShapeDtypeStruct((8, width), BF16),
            jax.ShapeDtypeStruct((width, hid), BF16),
            jax.ShapeDtypeStruct((hid, width), BF16),
        ),
        in_specs=[vmem, vmem, any_space, any_space],
        out_specs=(vmem, vmem, vmem, vmem),
        scratch_shapes=list(scratch.values()),
        compiler_params=pltpu.CompilerParams(
            collective_id=0, has_side_effects=True, vmem_limit_bytes=48 * 1024 * 1024
        ),
        name="ffn",
    )(tokens, grad_out, w_in, w_out)


def solution(mesh):
    ny, nz = mesh.shape["row"] // 2, mesh.shape["col"] // NX
    in_specs = (P("col", "row"), P("row", "col"), P("col", "row"), P("col", "row"))
    out_specs = (P("col", "row"), P("col", "row"), P("row", "col"), P("col", "row"))
    return jax.shard_map(
        functools.partial(local, ny, nz), mesh=mesh, in_specs=in_specs, out_specs=out_specs, check_vma=False
    )
```

```python
import functools
import math

import jax
import jax.numpy as jnp
from jax import lax
from jax.experimental import pallas as pl
from jax.experimental.pallas import tpu as pltpu
from jax.sharding import PartitionSpec as P

gelu_scale = math.sqrt(2.0 / math.pi)
MESH = pl.DeviceIdType.MESH
F32 = jnp.float32
BF16 = jnp.bfloat16

NX = 4
OFFSETS = (0, 1, 3, 2)
BACK = (0, 2, 1, 3)
GROUPS = ((0,), (1,), (2,), (3,))


def gelu_parts(hidden):
    inner = gelu_scale * (hidden + 0.044715 * hidden * hidden * hidden)
    tanh_value = jnp.tanh(inner)
    act_value = 0.5 * hidden * (1.0 + tanh_value)
    act_slope = 0.5 * (1.0 + tanh_value) + 0.5 * hidden * (
        1.0 - tanh_value * tanh_value
    ) * gelu_scale * (1.0 + 3.0 * 0.044715 * hidden * hidden)
    return (act_value, act_slope)


def mm_t(left, right):
    return lax.dot_general(left, right, (((1,), (1,)), ((), ())), preferred_element_type=F32)


def mm(left, right):
    return jnp.dot(left, right, preferred_element_type=F32)


def near_first(n):
    return sorted(range(1, n), key=lambda k: (min(k, n - k), k))


def far_first(n):
    return sorted(range(1, n), key=lambda k: (-min(k, n - k), k))


def scratch_list(ny, nz, width, hid):
    half, chunk = hid // 2, nz * 8
    s = {
        "win": pltpu.VMEM((width, hid), BF16),
        "wout": pltpu.VMEM((hid, width), BF16),
        "act_t": pltpu.VMEM((hid, NX * chunk), BF16),
        "tok_t": pltpu.VMEM((width, NX * chunk), BF16),
        "comb": pltpu.VMEM((NX, nz, 16, width), BF16),
        "tg": pltpu.VMEM((NX, 2, chunk, width), BF16),
        "actb": pltpu.VMEM((NX, chunk, hid), BF16),
        "ghb": pltpu.VMEM((NX, chunk, hid), BF16),
        "ds": pltpu.VMEM((NX, nz, 16, width), BF16),
        "dr": pltpu.VMEM((NX, nz, 16, width), BF16),
        "down": pltpu.VMEM((nz, 16, width), F32),
        "zs": pltpu.VMEM((nz, 16, width), BF16),
        "zr": pltpu.VMEM((nz, 16, width), BF16),
    }
    for g, slots in enumerate(GROUPS):
        n = len(slots)
        s[f"hk{g}"] = pltpu.VMEM((2, n * chunk, half), F32)
        s[f"xs{g}"] = pltpu.VMEM((2, n * chunk, half), F32)
        s[f"xr{g}"] = pltpu.VMEM((2, n * chunk, half), F32)
        s[f"bf{g}"] = pltpu.VMEM((ny, n * 16, half), F32)
        s[f"bs{g}"] = pltpu.VMEM((ny, n * 16, half), BF16)
        s[f"br{g}"] = pltpu.VMEM((ny, n * 16, half), BF16)
        s[f"cb{g}"] = pltpu.VMEM((2, ny, n * 16, half), BF16)
    dma = pltpu.SemaphoreType.DMA
    ng = len(GROUPS)
    s["w_sem"] = dma((4,))
    for name, shape in (
        ("az", (nz,)),
        ("ax", (NX, nz)),
        ("cx", (ng,)),
        ("by", (ng, ny)),
        ("cy", (ng, ny)),
        ("cf", (ng,)),
        ("dx", (NX, nz)),
        ("dz", (nz,)),
    ):
        s[name + "_s"] = dma(shape)
        s[name + "_r"] = dma(shape)
    return s


def kernel(ny, nz, names, tok_ref, grad_ref, win_hbm, wout_hbm, out_ref, gt_ref, gwin_ref, gwout_ref, *scratch):
    r = dict(zip(names, scratch))
    width, hid = r["win"].shape
    half, chunk = hid // 2, nz * 8
    row, col = lax.axis_index("row"), lax.axis_index("col")
    y, core = row // 2, lax.rem(row, 2)
    x, z = col // nz, lax.rem(col, nz)
    sibling = {"row": y * 2 + (1 - core), "col": col}

    def at_y(k):
        return {"row": lax.rem(y + k, ny) * 2 + core, "col": col}

    def at_x(k):
        return {"row": row, "col": lax.rem(x + k, NX) * nz + z}

    def at_z(k):
        return {"row": row, "col": x * nz + lax.rem(z + k, nz)}

    sent = []

    def send(src, dst, sem, send_at, recv_at, device):
        copy = pltpu.make_async_remote_copy(
            src_ref=src,
            dst_ref=dst,
            send_sem=r[sem + "_s"].at[send_at],
            recv_sem=r[sem + "_r"].at[recv_at],
            device_id=device,
            device_id_type=MESH,
        )
        copy.start()
        sent.append(copy)
        return copy

    weight_copies = []
    for h in range(2):
        start = pl.multiple_of((core if h == 0 else 1 - core) * half, half)
        weight_copies.append(
            pltpu.make_async_copy(
                win_hbm.at[:, pl.ds(start, half)], r["win"].at[:, pl.ds(h * half, half)], r["w_sem"].at[h]
            )
        )
        weight_copies.append(
            pltpu.make_async_copy(
                wout_hbm.at[pl.ds(start, half), :], r["wout"].at[pl.ds(h * half, half), :], r["w_sem"].at[2 + h]
            )
        )
    for copy in weight_copies:
        copy.start()

    barrier = pltpu.get_barrier_semaphore()
    partners = (
        [at_z(k) for k in range(1, nz)]
        + [at_x(k) for k in range(1, NX)]
        + [at_y(k) for k in range(1, ny)]
        + [sibling]
    )
    for device in partners:
        pl.semaphore_signal(barrier, inc=1, device_id=device, device_id_type=MESH)
    comb = r["comb"]
    comb[0, z] = jnp.concatenate([tok_ref[...].astype(F32), grad_ref[...].astype(F32)], axis=0).astype(BF16)
    pl.semaphore_wait(barrier, len(partners))

    az = {k: send(comb.at[0, z], comb.at[0, z], "az", k, nz - k, at_z(k)) for k in near_first(nz)}
    ax = {}

    def block_over_x(k):
        part = lax.rem(z + k, nz)
        for s in (3, 1, 2):
            ax[BACK[s], k] = send(
                comb.at[0, part], comb.at[BACK[s], part], "ax", (s, k), (BACK[s], k), at_x(OFFSETS[s])
            )

    block_over_x(0)
    for copy in weight_copies:
        copy.wait()
    for k in near_first(nz):
        az[nz - k].wait_recv()
        block_over_x(k)

    def split_chunk(s):
        block = comb[s].astype(F32)
        r["tg"][s, 0] = block[:, :8, :].reshape(chunk, width).astype(BF16)
        r["tg"][s, 1] = block[:, 8:, :].reshape(chunk, width).astype(BF16)

    live = {}

    def rows_of(name, part, slots):
        return jnp.concatenate([r[name][s, part] for s in slots], axis=0)

    def first_products(g):
        slots = GROUPS[g]
        for s in slots:
            if s:
                for k in range(nz):
                    ax[s, k].wait_recv()
            split_chunk(s)
        hidden = mm(rows_of("tg", 0, slots), r["win"][...])
        grad_act = mm_t(rows_of("tg", 1, slots), r["wout"][...])
        for i, value in enumerate((hidden, grad_act)):
            r[f"xs{g}"][i] = value[:, half:]
            r[f"hk{g}"][i] = value[:, :half]
        live["cx", g] = send(r[f"xs{g}"], r[f"xr{g}"], "cx", g, g, sibling)

    def terms_over_y(g):
        n = len(GROUPS[g])
        live["cx", g].wait_recv()
        both = [r[f"hk{g}"][i] + r[f"xr{g}"][i] for i in range(2)]
        for d in range(ny):
            parts = []
            for i in range(n):
                for j in range(2):
                    at = i * chunk + d * 8
                    parts.append(both[j][at : at + 8])
            value = jnp.concatenate(parts, axis=0)
            r[f"bf{g}"][d] = value
            r[f"bs{g}"][d] = value.astype(BF16)
        live["by", g] = [
            send(r[f"bs{g}"].at[lax.rem(y + k, ny)], r[f"br{g}"].at[ny - k], "by", (g, k), (g, ny - k), at_y(k))
            for k in far_first(ny)
        ]

    def activate(g):
        n = len(GROUPS[g])
        total = r[f"bf{g}"][y]
        for copy in live["by", g]:
            copy.wait_recv()
        for k in range(1, ny):
            total = total + r[f"br{g}"][k].astype(F32)
        total = total.reshape(n, 2, 8, half)
        act_value, act_slope = gelu_parts(total[:, 0])
        grad_hidden = total[:, 1] * act_slope
        both = jnp.stack([act_value, grad_hidden], axis=1).reshape(n * 16, half)
        r[f"cb{g}"][0, y] = both.astype(BF16)
        own = r[f"cb{g}"].at[0, y]
        live["cy", g] = [send(own, own, "cy", (g, k), (g, ny - k), at_y(k)) for k in far_first(ny)]

    def forward(g):
        for copy in live["cy", g]:
            copy.wait_recv()
        live["cf", g] = send(r[f"cb{g}"].at[0], r[f"cb{g}"].at[1], "cf", g, g, sibling)

    def second_products(g):
        slots = GROUPS[g]
        n = len(slots)
        live["cf", g].wait_recv()
        for h in range(2):
            got = r[f"cb{g}"][h].astype(F32).reshape(ny, n, 2, 8, half)
            for i, s in enumerate(slots):
                r["actb"][s, :, h * half : (h + 1) * half] = got[:, i, 0].reshape(chunk, half).astype(BF16)
                r["ghb"][s, :, h * half : (h + 1) * half] = got[:, i, 1].reshape(chunk, half).astype(BF16)
        first, last = slots[0], slots[-1] + 1
        act = r["actb"][first:last].reshape(n * chunk, hid)
        grad_hidden = r["ghb"][first:last].reshape(n * chunk, hid)
        out_part = mm(act, r["wout"][...])
        grad_part = mm_t(grad_hidden, r["win"][...])
        for i, s in enumerate(slots):
            for d in range(nz):
                at = i * chunk + d * 8
                part = jnp.concatenate([out_part[at : at + 8], grad_part[at : at + 8]], axis=0)
                if s:
                    r["ds"][s, d] = part.astype(BF16)
                else:
                    r["down"][d] = part
        for k in (*far_first(nz), 0):
            part = lax.rem(z + k, nz)
            for s in slots:
                if s:
                    live["dx", BACK[s], k] = send(
                        r["ds"].at[s, part], r["dr"].at[BACK[s], part], "dx", (s, k), (BACK[s], k), at_x(OFFSETS[s])
                    )

    first_products(0)
    terms_over_y(0)
    first_products(1)
    first_products(2)
    terms_over_y(1)
    first_products(3)
    terms_over_y(2)
    terms_over_y(3)
    activate(0)
    activate(1)
    forward(0)
    activate(2)
    second_products(0)
    activate(3)
    forward(1)
    forward(2)
    second_products(1)
    forward(3)
    second_products(2)
    second_products(3)

    tile = min(256, half)
    tokens_all = rows_of("tg", 0, range(NX))
    grad_all = rows_of("tg", 1, range(NX))
    r["act_t"][...] = r["actb"][...].reshape(NX * chunk, hid).T
    r["tok_t"][...] = tokens_all.T
    grad_hidden_all = r["ghb"][...].reshape(NX * chunk, hid)
    for h in range(2):
        start = pl.multiple_of((core if h == 0 else 1 - core) * half, half)
        gwout_ref[pl.ds(start, half), :] = mm(
            r["act_t"][h * half : (h + 1) * half, :], grad_all
        ).astype(BF16)
        gwin_ref[:, pl.ds(start, half)] = mm(
            r["tok_t"][...], grad_hidden_all[:, h * half : (h + 1) * half]
        ).astype(BF16)

    def sum_over_x(k):
        part = lax.rem(z + k, nz)
        value = r["down"][part]
        for s in (1, 2, 3):
            live["dx", s, k].wait_recv()
        for s in (1, 2, 3):
            value = value + r["dr"][s, part].astype(F32)
        return value

    dz = {}
    for k in far_first(nz):
        part = lax.rem(z + k, nz)
        r["zs"][part] = sum_over_x(k).astype(BF16)
        dz[k] = send(r["zs"].at[part], r["zr"].at[nz - k], "dz", k, nz - k, at_z(k))
    total = sum_over_x(0)
    for k in far_first(nz):
        dz[nz - k].wait_recv()
        total = total + r["zr"][k].astype(F32)
    out_ref[...] = total[:8].astype(BF16)
    gt_ref[...] = total[8:].astype(BF16)
    for copy in sent:
        copy.wait_send()


def local(ny, nz, tokens, w_in, w_out, grad_out):
    width, hid = w_in.shape
    scratch = scratch_list(ny, nz, width, hid)
    vmem = pl.BlockSpec(memory_space=pltpu.VMEM)
    hbm = pl.BlockSpec(memory_space=pltpu.HBM)
    return pl.pallas_call(
        functools.partial(kernel, ny, nz, tuple(scratch)),
        out_shape=(
            jax.ShapeDtypeStruct((8, width), BF16),
            jax.ShapeDtypeStruct((8, width), BF16),
            jax.ShapeDtypeStruct((width, hid), BF16),
            jax.ShapeDtypeStruct((hid, width), BF16),
        ),
        in_specs=[vmem, vmem, hbm, hbm],
        out_specs=(vmem, vmem, vmem, vmem),
        scratch_shapes=list(scratch.values()),
        compiler_params=pltpu.CompilerParams(
            collective_id=0, has_side_effects=True, vmem_limit_bytes=51 * 1024 * 1024
        ),
        name="ffn",
    )(tokens, grad_out, w_in, w_out)


def solution(mesh):
    ny, nz = mesh.shape["row"] // 2, mesh.shape["col"] // NX
    in_specs = (P("col", "row"), P("row", "col"), P("col", "row"), P("col", "row"))
    out_specs = (P("col", "row"), P("col", "row"), P("row", "col"), P("col", "row"))
    return jax.shard_map(
        functools.partial(local, ny, nz), mesh=mesh, in_specs=in_specs, out_specs=out_specs, check_vma=False
    )
```

```python
import functools
import math

import jax
import jax.numpy as jnp
from jax import lax
from jax.experimental import pallas as pl
from jax.experimental.pallas import tpu as pltpu
from jax.sharding import PartitionSpec as P

gelu_scale = math.sqrt(2.0 / math.pi)
MESH = pl.DeviceIdType.MESH
F32 = jnp.float32
BF16 = jnp.bfloat16

NX = 4
NEAR_LAG = 7
OFFSETS = (0, 1, 3, 2)
BACK = (0, 2, 1, 3)
GROUPS = ((0,), (1,), (2,), (3,))


SEQUENCE = ((0, 0), (1, 0), (0, 3), (1, 3), (2, 0), (0, 1), (0, 2), (1, 1), (1, 2), (3, 0), (2, 3), (4, 0), (2, 1), (2, 2), (3, 3), (4, 3), (3, 1), (3, 2), (4, 1), (4, 2))


def gelu_parts(hidden):
    inner = gelu_scale * (hidden + 0.044715 * hidden * hidden * hidden)
    tanh_value = jnp.tanh(inner)
    act_value = 0.5 * hidden * (1.0 + tanh_value)
    act_slope = 0.5 * (1.0 + tanh_value) + 0.5 * hidden * (
        1.0 - tanh_value * tanh_value
    ) * gelu_scale * (1.0 + 3.0 * 0.044715 * hidden * hidden)
    return (act_value, act_slope)


def mm_t(left, right):
    return lax.dot_general(left, right, (((1,), (1,)), ((), ())), preferred_element_type=F32)


def mm(left, right):
    return jnp.dot(left, right, preferred_element_type=F32)


def near_first(n):
    return sorted(range(1, n), key=lambda k: (min(k, n - k), k))


def far_first(n):
    return sorted(range(1, n), key=lambda k: (-min(k, n - k), k))


def scratch_list(ny, nz, width, hid):
    half, chunk = hid // 2, nz * 8
    s = {
        "win": pltpu.VMEM((width, hid), BF16),
        "wout": pltpu.VMEM((hid, width), BF16),
        "act_t": pltpu.VMEM((hid, NX * chunk), BF16),
        "tok_t": pltpu.VMEM((width, NX * chunk), BF16),
        "comb": pltpu.VMEM((NX, nz, 16, width), BF16),
        "tg": pltpu.VMEM((NX, 2, chunk, width), BF16),
        "actb": pltpu.VMEM((NX, chunk, hid), BF16),
        "ghb": pltpu.VMEM((NX, chunk, hid), BF16),
        "ds": pltpu.VMEM((NX, nz, 16, width), BF16),
        "dr": pltpu.VMEM((NX, nz, 16, width), BF16),
        "down": pltpu.VMEM((nz, 16, width), F32),
        "zs": pltpu.VMEM((nz, 16, width), BF16),
        "zr": pltpu.VMEM((nz, 16, width), BF16),
    }
    for g, slots in enumerate(GROUPS):
        n = len(slots)
        s[f"hk{g}"] = pltpu.VMEM((2, n * chunk, half), F32)
        s[f"xs{g}"] = pltpu.VMEM((2, n * chunk, half), F32)
        s[f"xr{g}"] = pltpu.VMEM((2, n * chunk, half), F32)
        s[f"bf{g}"] = pltpu.VMEM((ny, n * 16, half), F32)
        s[f"bs{g}"] = pltpu.VMEM((ny, n * 16, half), BF16)
        s[f"br{g}"] = pltpu.VMEM((ny, n * 16, half), BF16)
        s[f"cb{g}"] = pltpu.VMEM((2, ny, n * 16, half), BF16)
    dma = pltpu.SemaphoreType.DMA
    ng = len(GROUPS)
    s["w_sem"] = dma((4,))
    for name, shape in (
        ("az", (nz,)),
        ("ax", (NX, nz)),
        ("cx", (ng,)),
        ("by", (ng, ny)),
        ("cy", (ng, ny)),
        ("cf", (ng,)),
        ("dx", (NX, nz)),
        ("dz", (nz,)),
    ):
        s[name + "_s"] = dma(shape)
        s[name + "_r"] = dma(shape)
    return s


def kernel(ny, nz, names, tok_ref, grad_ref, win_hbm, wout_hbm, out_ref, gt_ref, gwin_ref, gwout_ref, *scratch):
    r = dict(zip(names, scratch))
    width, hid = r["win"].shape
    half, chunk = hid // 2, nz * 8
    row, col = lax.axis_index("row"), lax.axis_index("col")
    y, core = row // 2, lax.rem(row, 2)
    x, z = col // nz, lax.rem(col, nz)
    sibling = {"row": y * 2 + (1 - core), "col": col}

    def at_y(k):
        return {"row": lax.rem(y + k, ny) * 2 + core, "col": col}

    def at_x(k):
        return {"row": row, "col": lax.rem(x + k, NX) * nz + z}

    def at_z(k):
        return {"row": row, "col": x * nz + lax.rem(z + k, nz)}

    sent = []

    def send(src, dst, sem, send_at, recv_at, device):
        copy = pltpu.make_async_remote_copy(
            src_ref=src,
            dst_ref=dst,
            send_sem=r[sem + "_s"].at[send_at],
            recv_sem=r[sem + "_r"].at[recv_at],
            device_id=device,
            device_id_type=MESH,
        )
        copy.start()
        sent.append(copy)
        return copy

    weight_copies = []
    for h in range(2):
        start = pl.multiple_of((core if h == 0 else 1 - core) * half, half)
        weight_copies.append(
            pltpu.make_async_copy(
                win_hbm.at[:, pl.ds(start, half)], r["win"].at[:, pl.ds(h * half, half)], r["w_sem"].at[h]
            )
        )
        weight_copies.append(
            pltpu.make_async_copy(
                wout_hbm.at[pl.ds(start, half), :], r["wout"].at[pl.ds(h * half, half), :], r["w_sem"].at[2 + h]
            )
        )
    for copy in weight_copies:
        copy.start()

    barrier = pltpu.get_barrier_semaphore()
    partners = (
        [at_z(k) for k in range(1, nz)]
        + [at_x(k) for k in range(1, NX)]
        + [at_y(k) for k in range(1, ny)]
        + [sibling]
    )
    for device in partners:
        pl.semaphore_signal(barrier, inc=1, device_id=device, device_id_type=MESH)
    comb = r["comb"]
    comb[0, z] = jnp.concatenate([tok_ref[...].astype(F32), grad_ref[...].astype(F32)], axis=0).astype(BF16)
    pl.semaphore_wait(barrier, len(partners))

    az = {k: send(comb.at[0, z], comb.at[0, z], "az", k, nz - k, at_z(k)) for k in near_first(nz)}
    ax = {}

    def block_over_x(k, slots):
        part = lax.rem(z + k, nz)
        for s in slots:
            ax[BACK[s], k] = send(
                comb.at[0, part], comb.at[BACK[s], part], "ax", (s, k), (BACK[s], k), at_x(OFFSETS[s])
            )

    block_over_x(0, (3, 1, 2))
    for copy in weight_copies:
        copy.wait()
    order = near_first(nz)
    for i, k in enumerate(order):
        az[nz - k].wait_recv()
        block_over_x(k, (3,))
        if i >= NEAR_LAG:
            block_over_x(order[i - NEAR_LAG], (1, 2))
    for k in order[len(order) - NEAR_LAG :]:
        block_over_x(k, (1, 2))

    def split_chunk(s):
        block = comb[s].astype(F32)
        r["tg"][s, 0] = block[:, :8, :].reshape(chunk, width).astype(BF16)
        r["tg"][s, 1] = block[:, 8:, :].reshape(chunk, width).astype(BF16)

    live = {}

    def rows_of(name, part, slots):
        return jnp.concatenate([r[name][s, part] for s in slots], axis=0)

    def first_products(g):
        slots = GROUPS[g]
        for s in slots:
            if s:
                for k in range(nz):
                    ax[s, k].wait_recv()
            split_chunk(s)
        hidden = mm(rows_of("tg", 0, slots), r["win"][...])
        grad_act = mm_t(rows_of("tg", 1, slots), r["wout"][...])
        for i, value in enumerate((hidden, grad_act)):
            r[f"xs{g}"][i] = value[:, half:]
            r[f"hk{g}"][i] = value[:, :half]
        live["cx", g] = send(r[f"xs{g}"], r[f"xr{g}"], "cx", g, g, sibling)

    def terms_over_y(g):
        n = len(GROUPS[g])
        live["cx", g].wait_recv()
        both = [r[f"hk{g}"][i] + r[f"xr{g}"][i] for i in range(2)]
        for d in range(ny):
            parts = []
            for i in range(n):
                for j in range(2):
                    at = i * chunk + d * 8
                    parts.append(both[j][at : at + 8])
            value = jnp.concatenate(parts, axis=0)
            r[f"bf{g}"][d] = value
            r[f"bs{g}"][d] = value.astype(BF16)
        live["by", g] = [
            send(r[f"bs{g}"].at[lax.rem(y + k, ny)], r[f"br{g}"].at[ny - k], "by", (g, k), (g, ny - k), at_y(k))
            for k in far_first(ny)
        ]

    def activate(g):
        n = len(GROUPS[g])
        total = r[f"bf{g}"][y]
        for copy in live["by", g]:
            copy.wait_recv()
        for k in range(1, ny):
            total = total + r[f"br{g}"][k].astype(F32)
        total = total.reshape(n, 2, 8, half)
        act_value, act_slope = gelu_parts(total[:, 0])
        grad_hidden = total[:, 1] * act_slope
        both = jnp.stack([act_value, grad_hidden], axis=1).reshape(n * 16, half)
        r[f"cb{g}"][0, y] = both.astype(BF16)
        own = r[f"cb{g}"].at[0, y]
        live["cy", g] = [send(own, own, "cy", (g, k), (g, ny - k), at_y(k)) for k in far_first(ny)]

    def forward(g):
        for copy in live["cy", g]:
            copy.wait_recv()
        live["cf", g] = send(r[f"cb{g}"].at[0], r[f"cb{g}"].at[1], "cf", g, g, sibling)

    def second_products(g):
        slots = GROUPS[g]
        n = len(slots)
        live["cf", g].wait_recv()
        for h in range(2):
            got = r[f"cb{g}"][h].astype(F32).reshape(ny, n, 2, 8, half)
            for i, s in enumerate(slots):
                r["actb"][s, :, h * half : (h + 1) * half] = got[:, i, 0].reshape(chunk, half).astype(BF16)
                r["ghb"][s, :, h * half : (h + 1) * half] = got[:, i, 1].reshape(chunk, half).astype(BF16)
        first, last = slots[0], slots[-1] + 1
        act = r["actb"][first:last].reshape(n * chunk, hid)
        grad_hidden = r["ghb"][first:last].reshape(n * chunk, hid)
        out_part = mm(act, r["wout"][...])
        grad_part = mm_t(grad_hidden, r["win"][...])
        for i, s in enumerate(slots):
            for d in range(nz):
                at = i * chunk + d * 8
                part = jnp.concatenate([out_part[at : at + 8], grad_part[at : at + 8]], axis=0)
                if s:
                    r["ds"][s, d] = part.astype(BF16)
                else:
                    r["down"][d] = part
        for k in (*far_first(nz), 0):
            part = lax.rem(z + k, nz)
            for s in slots:
                if s:
                    live["dx", BACK[s], k] = send(
                        r["ds"].at[s, part], r["dr"].at[BACK[s], part], "dx", (s, k), (BACK[s], k), at_x(OFFSETS[s])
                    )

    for step, g in SEQUENCE:
        (first_products, terms_over_y, activate, forward, second_products)[step](g)

    tile = min(256, half)
    tokens_all = rows_of("tg", 0, range(NX))
    grad_all = rows_of("tg", 1, range(NX))
    r["act_t"][...] = r["actb"][...].reshape(NX * chunk, hid).T
    r["tok_t"][...] = tokens_all.T
    grad_hidden_all = r["ghb"][...].reshape(NX * chunk, hid)
    for h in range(2):
        start = pl.multiple_of((core if h == 0 else 1 - core) * half, half)
        gwout_ref[pl.ds(start, half), :] = mm(
            r["act_t"][h * half : (h + 1) * half, :], grad_all
        ).astype(BF16)
        gwin_ref[:, pl.ds(start, half)] = mm(
            r["tok_t"][...], grad_hidden_all[:, h * half : (h + 1) * half]
        ).astype(BF16)

    def sum_over_x(k):
        part = lax.rem(z + k, nz)
        value = r["down"][part]
        for s in (1, 2, 3):
            live["dx", s, k].wait_recv()
        for s in (1, 2, 3):
            value = value + r["dr"][s, part].astype(F32)
        return value

    dz = {}
    for k in far_first(nz):
        part = lax.rem(z + k, nz)
        r["zs"][part] = sum_over_x(k).astype(BF16)
        dz[k] = send(r["zs"].at[part], r["zr"].at[nz - k], "dz", k, nz - k, at_z(k))
    total = sum_over_x(0)
    for k in far_first(nz):
        dz[nz - k].wait_recv()
        total = total + r["zr"][k].astype(F32)
    out_ref[...] = total[:8].astype(BF16)
    gt_ref[...] = total[8:].astype(BF16)
    for copy in sent:
        copy.wait_send()


def local(ny, nz, tokens, w_in, w_out, grad_out):
    width, hid = w_in.shape
    scratch = scratch_list(ny, nz, width, hid)
    vmem = pl.BlockSpec(memory_space=pltpu.VMEM)
    hbm = pl.BlockSpec(memory_space=pltpu.HBM)
    results = pl.pallas_call(
        functools.partial(kernel, ny, nz, tuple(scratch)),
        out_shape=(
            jax.ShapeDtypeStruct((8, width), BF16),
            jax.ShapeDtypeStruct((8, width), BF16),
            jax.ShapeDtypeStruct((width, hid), BF16),
            jax.ShapeDtypeStruct((hid, width), BF16),
        ),
        in_specs=[vmem, vmem, hbm, hbm],
        out_specs=(vmem, vmem, vmem, vmem),
        scratch_shapes=list(scratch.values()),
        compiler_params=pltpu.CompilerParams(
            collective_id=0, has_side_effects=True, vmem_limit_bytes=51 * 1024 * 1024
        ),
        name="ffn",
    )(tokens, grad_out, w_in, w_out)
    anywhere = pl.BlockSpec(memory_space=pl.ANY)
    return pl.pallas_call(
        write_out,
        out_shape=tuple(jax.ShapeDtypeStruct(a.shape, a.dtype) for a in results),
        in_specs=[anywhere] * 4,
        out_specs=(anywhere,) * 4,
        scratch_shapes=[pltpu.SemaphoreType.DMA((4,))],
        compiler_params=pltpu.CompilerParams(vmem_limit_bytes=1024 * 1024),
        name="write_out",
    )(*results)


def write_out(*refs):
    sources, targets, sem = refs[:4], refs[4:8], refs[8]
    copies = [pltpu.make_async_copy(a, b, sem.at[i]) for i, (a, b) in enumerate(zip(sources, targets))]
    for copy in copies[::-1]:
        copy.start()
    for copy in copies:
        copy.wait()


def solution(mesh):
    ny, nz = mesh.shape["row"] // 2, mesh.shape["col"] // NX
    in_specs = (P("col", "row"), P("row", "col"), P("col", "row"), P("col", "row"))
    out_specs = (P("col", "row"), P("col", "row"), P("row", "col"), P("col", "row"))
    return jax.shard_map(
        functools.partial(local, ny, nz), mesh=mesh, in_specs=in_specs, out_specs=out_specs, check_vma=False
    )
```

```python
import functools
import math

import jax
import jax.numpy as jnp
from jax import lax
from jax.experimental import pallas as pl
from jax.experimental.pallas import tpu as pltpu
from jax.sharding import PartitionSpec as P

gelu_scale = math.sqrt(2.0 / math.pi)
MESH = pl.DeviceIdType.MESH
F32 = jnp.float32
BF16 = jnp.bfloat16

NX = 4
NEAR_LAG = 7
OFFSETS = (0, 1, 3, 2)
BACK = (0, 2, 1, 3)
GROUPS = ((0,), (1,), (2,), (3,))


SEQUENCE = ((0, 0), (1, 0), (0, 3), (1, 3), (2, 0), (0, 1), (0, 2), (1, 1), (1, 2), (3, 0), (2, 3), (4, 0), (2, 1), (2, 2), (3, 3), (4, 3), (3, 1), (3, 2), (4, 1), (4, 2))


def gelu_parts(hidden):
    inner = gelu_scale * (hidden + 0.044715 * hidden * hidden * hidden)
    tanh_value = jnp.tanh(inner)
    act_value = 0.5 * hidden * (1.0 + tanh_value)
    act_slope = 0.5 * (1.0 + tanh_value) + 0.5 * hidden * (
        1.0 - tanh_value * tanh_value
    ) * gelu_scale * (1.0 + 3.0 * 0.044715 * hidden * hidden)
    return (act_value, act_slope)


def mm_t(left, right):
    return lax.dot_general(left, right, (((1,), (1,)), ((), ())), preferred_element_type=F32)


def mm(left, right):
    return jnp.dot(left, right, preferred_element_type=F32)


def near_first(n):
    return sorted(range(1, n), key=lambda k: (min(k, n - k), k))


def far_first(n):
    return sorted(range(1, n), key=lambda k: (-min(k, n - k), k))


def scratch_list(ny, nz, width, hid):
    half, chunk = hid // 2, nz * 8
    s = {
        "win": pltpu.VMEM((width, hid), BF16),
        "wout": pltpu.VMEM((hid, width), BF16),
        "act_t": pltpu.VMEM((hid, NX * chunk), BF16),
        "tok_t": pltpu.VMEM((width, NX * chunk), BF16),
        "comb": pltpu.VMEM((NX, nz, 16, width), BF16),
        "tg": pltpu.VMEM((NX, 2, chunk, width), BF16),
        "actb": pltpu.VMEM((NX, chunk, hid), BF16),
        "ghb": pltpu.VMEM((NX, chunk, hid), BF16),
        "ds": pltpu.VMEM((NX, nz, 16, width), BF16),
        "dr": pltpu.VMEM((NX, nz, 16, width), BF16),
        "down": pltpu.VMEM((nz, 16, width), F32),
        "zs": pltpu.VMEM((nz, 16, width), BF16),
        "zr": pltpu.VMEM((nz, 16, width), BF16),
    }
    for g, slots in enumerate(GROUPS):
        n = len(slots)
        s[f"hk{g}"] = pltpu.VMEM((2, n * chunk, half), F32)
        s[f"xs{g}"] = pltpu.VMEM((2, n * chunk, half), F32)
        s[f"xr{g}"] = pltpu.VMEM((2, n * chunk, half), F32)
        s[f"bf{g}"] = pltpu.VMEM((ny, n * 16, half), F32)
        s[f"bs{g}"] = pltpu.VMEM((ny, n * 16, half), BF16)
        s[f"br{g}"] = pltpu.VMEM((ny, n * 16, half), BF16)
        s[f"cb{g}"] = pltpu.VMEM((2, ny, n * 16, half), BF16)
    dma = pltpu.SemaphoreType.DMA
    ng = len(GROUPS)
    s["w_sem"] = dma((4,))
    for name, shape in (
        ("az", (nz,)),
        ("ax", (NX, nz)),
        ("cx", (ng,)),
        ("by", (ng, ny)),
        ("cy", (ng, ny)),
        ("cf", (ng,)),
        ("dx", (NX, nz)),
        ("dz", (nz,)),
    ):
        s[name + "_s"] = dma(shape)
        s[name + "_r"] = dma(shape)
    return s


def kernel(ny, nz, names, tok_ref, grad_ref, win_hbm, wout_hbm, out_ref, gt_ref, gwin_ref, gwout_ref, *scratch):
    r = dict(zip(names, scratch))
    width, hid = r["win"].shape
    half, chunk = hid // 2, nz * 8
    row, col = lax.axis_index("row"), lax.axis_index("col")
    y, core = row // 2, lax.rem(row, 2)
    x, z = col // nz, lax.rem(col, nz)
    sibling = {"row": y * 2 + (1 - core), "col": col}

    def at_y(k):
        return {"row": lax.rem(y + k, ny) * 2 + core, "col": col}

    def at_x(k):
        return {"row": row, "col": lax.rem(x + k, NX) * nz + z}

    def at_z(k):
        return {"row": row, "col": x * nz + lax.rem(z + k, nz)}

    sent = []

    def send(src, dst, sem, send_at, recv_at, device):
        copy = pltpu.make_async_remote_copy(
            src_ref=src,
            dst_ref=dst,
            send_sem=r[sem + "_s"].at[send_at],
            recv_sem=r[sem + "_r"].at[recv_at],
            device_id=device,
            device_id_type=MESH,
        )
        copy.start()
        sent.append(copy)
        return copy

    weight_copies = []
    for h in range(2):
        start = pl.multiple_of((core if h == 0 else 1 - core) * half, half)
        weight_copies.append(
            pltpu.make_async_copy(
                win_hbm.at[:, pl.ds(start, half)], r["win"].at[:, pl.ds(h * half, half)], r["w_sem"].at[h]
            )
        )
        weight_copies.append(
            pltpu.make_async_copy(
                wout_hbm.at[pl.ds(start, half), :], r["wout"].at[pl.ds(h * half, half), :], r["w_sem"].at[2 + h]
            )
        )
    for copy in weight_copies:
        copy.start()

    barrier = pltpu.get_barrier_semaphore()
    partners = (
        [at_z(k) for k in range(1, nz)]
        + [at_x(k) for k in range(1, NX)]
        + [at_y(k) for k in range(1, ny)]
        + [sibling]
    )
    for device in partners:
        pl.semaphore_signal(barrier, inc=1, device_id=device, device_id_type=MESH)
    comb = r["comb"]
    comb[0, z] = jnp.concatenate([tok_ref[...].astype(F32), grad_ref[...].astype(F32)], axis=0).astype(BF16)
    pl.semaphore_wait(barrier, len(partners))

    az = {k: send(comb.at[0, z], comb.at[0, z], "az", k, nz - k, at_z(k)) for k in near_first(nz)}
    ax = {}

    def block_over_x(k, slots):
        part = lax.rem(z + k, nz)
        for s in slots:
            ax[BACK[s], k] = send(
                comb.at[0, part], comb.at[BACK[s], part], "ax", (s, k), (BACK[s], k), at_x(OFFSETS[s])
            )

    block_over_x(0, (3, 1, 2))
    order = near_first(nz)
    for i, k in enumerate(order):
        az[nz - k].wait_recv()
        block_over_x(k, (3,))
        if i >= NEAR_LAG:
            block_over_x(order[i - NEAR_LAG], (1, 2))
    for k in order[len(order) - NEAR_LAG :]:
        block_over_x(k, (1, 2))
    for copy in weight_copies:
        copy.wait()

    def split_chunk(s):
        block = comb[s].astype(F32)
        r["tg"][s, 0] = block[:, :8, :].reshape(chunk, width).astype(BF16)
        r["tg"][s, 1] = block[:, 8:, :].reshape(chunk, width).astype(BF16)

    live = {}

    def rows_of(name, part, slots):
        return jnp.concatenate([r[name][s, part] for s in slots], axis=0)

    def first_products(g):
        slots = GROUPS[g]
        for s in slots:
            if s:
                for k in range(nz):
                    ax[s, k].wait_recv()
            split_chunk(s)
        hidden = mm(rows_of("tg", 0, slots), r["win"][...])
        grad_act = mm_t(rows_of("tg", 1, slots), r["wout"][...])
        for i, value in enumerate((hidden, grad_act)):
            r[f"xs{g}"][i] = value[:, half:]
            r[f"hk{g}"][i] = value[:, :half]
        live["cx", g] = send(r[f"xs{g}"], r[f"xr{g}"], "cx", g, g, sibling)

    def terms_over_y(g):
        n = len(GROUPS[g])
        live["cx", g].wait_recv()
        both = [r[f"hk{g}"][i] + r[f"xr{g}"][i] for i in range(2)]
        for d in range(ny):
            parts = []
            for i in range(n):
                for j in range(2):
                    at = i * chunk + d * 8
                    parts.append(both[j][at : at + 8])
            value = jnp.concatenate(parts, axis=0)
            r[f"bf{g}"][d] = value
            r[f"bs{g}"][d] = value.astype(BF16)
        live["by", g] = [
            send(r[f"bs{g}"].at[lax.rem(y + k, ny)], r[f"br{g}"].at[ny - k], "by", (g, k), (g, ny - k), at_y(k))
            for k in far_first(ny)
        ]

    def activate(g):
        n = len(GROUPS[g])
        total = r[f"bf{g}"][y]
        for copy in live["by", g]:
            copy.wait_recv()
        for k in range(1, ny):
            total = total + r[f"br{g}"][k].astype(F32)
        total = total.reshape(n, 2, 8, half)
        act_value, act_slope = gelu_parts(total[:, 0])
        grad_hidden = total[:, 1] * act_slope
        both = jnp.stack([act_value, grad_hidden], axis=1).reshape(n * 16, half)
        r[f"cb{g}"][0, y] = both.astype(BF16)
        own = r[f"cb{g}"].at[0, y]
        live["cy", g] = [send(own, own, "cy", (g, k), (g, ny - k), at_y(k)) for k in far_first(ny)]

    def forward(g):
        for copy in live["cy", g]:
            copy.wait_recv()
        live["cf", g] = send(r[f"cb{g}"].at[0], r[f"cb{g}"].at[1], "cf", g, g, sibling)

    def second_products(g):
        slots = GROUPS[g]
        n = len(slots)
        live["cf", g].wait_recv()
        for h in range(2):
            got = r[f"cb{g}"][h].astype(F32).reshape(ny, n, 2, 8, half)
            for i, s in enumerate(slots):
                r["actb"][s, :, h * half : (h + 1) * half] = got[:, i, 0].reshape(chunk, half).astype(BF16)
                r["ghb"][s, :, h * half : (h + 1) * half] = got[:, i, 1].reshape(chunk, half).astype(BF16)
        first, last = slots[0], slots[-1] + 1
        act = r["actb"][first:last].reshape(n * chunk, hid)
        grad_hidden = r["ghb"][first:last].reshape(n * chunk, hid)
        out_part = mm(act, r["wout"][...])
        grad_part = mm_t(grad_hidden, r["win"][...])
        for i, s in enumerate(slots):
            for d in range(nz):
                at = i * chunk + d * 8
                part = jnp.concatenate([out_part[at : at + 8], grad_part[at : at + 8]], axis=0)
                if s:
                    r["ds"][s, d] = part.astype(BF16)
                else:
                    r["down"][d] = part
        for k in (*far_first(nz), 0):
            part = lax.rem(z + k, nz)
            for s in slots:
                if s:
                    live["dx", BACK[s], k] = send(
                        r["ds"].at[s, part], r["dr"].at[BACK[s], part], "dx", (s, k), (BACK[s], k), at_x(OFFSETS[s])
                    )

    for step, g in SEQUENCE:
        (first_products, terms_over_y, activate, forward, second_products)[step](g)

    tile = min(256, half)
    tokens_all = rows_of("tg", 0, range(NX))
    grad_all = rows_of("tg", 1, range(NX))
    r["act_t"][...] = r["actb"][...].reshape(NX * chunk, hid).T
    r["tok_t"][...] = tokens_all.T
    grad_hidden_all = r["ghb"][...].reshape(NX * chunk, hid)
    for h in range(2):
        start = pl.multiple_of((core if h == 0 else 1 - core) * half, half)
        gwout_ref[pl.ds(start, half), :] = mm(
            r["act_t"][h * half : (h + 1) * half, :], grad_all
        ).astype(BF16)
        gwin_ref[:, pl.ds(start, half)] = mm(
            r["tok_t"][...], grad_hidden_all[:, h * half : (h + 1) * half]
        ).astype(BF16)

    def sum_over_x(k):
        part = lax.rem(z + k, nz)
        value = r["down"][part]
        for s in (1, 2, 3):
            live["dx", s, k].wait_recv()
        for s in (1, 2, 3):
            value = value + r["dr"][s, part].astype(F32)
        return value

    dz = {}
    for k in far_first(nz):
        part = lax.rem(z + k, nz)
        r["zs"][part] = sum_over_x(k).astype(BF16)
        dz[k] = send(r["zs"].at[part], r["zr"].at[nz - k], "dz", k, nz - k, at_z(k))
    total = sum_over_x(0)
    for k in far_first(nz):
        dz[nz - k].wait_recv()
        total = total + r["zr"][k].astype(F32)
    out_ref[...] = total[:8].astype(BF16)
    gt_ref[...] = total[8:].astype(BF16)
    for copy in sent:
        copy.wait_send()


def local(ny, nz, tokens, w_in, w_out, grad_out):
    width, hid = w_in.shape
    scratch = scratch_list(ny, nz, width, hid)
    vmem = pl.BlockSpec(memory_space=pltpu.VMEM)
    hbm = pl.BlockSpec(memory_space=pltpu.HBM)
    results = pl.pallas_call(
        functools.partial(kernel, ny, nz, tuple(scratch)),
        out_shape=(
            jax.ShapeDtypeStruct((8, width), BF16),
            jax.ShapeDtypeStruct((8, width), BF16),
            jax.ShapeDtypeStruct((width, hid), BF16),
            jax.ShapeDtypeStruct((hid, width), BF16),
        ),
        in_specs=[vmem, vmem, hbm, hbm],
        out_specs=(vmem, vmem, vmem, vmem),
        scratch_shapes=list(scratch.values()),
        compiler_params=pltpu.CompilerParams(
            collective_id=0, has_side_effects=True, vmem_limit_bytes=51 * 1024 * 1024
        ),
        name="ffn",
    )(tokens, grad_out, w_in, w_out)
    anywhere = pl.BlockSpec(memory_space=pl.ANY)
    return pl.pallas_call(
        write_out,
        out_shape=tuple(jax.ShapeDtypeStruct(a.shape, a.dtype) for a in results),
        in_specs=[anywhere] * 4,
        out_specs=(anywhere,) * 4,
        scratch_shapes=[pltpu.SemaphoreType.DMA((4,))],
        compiler_params=pltpu.CompilerParams(vmem_limit_bytes=1024 * 1024),
        name="write_out",
    )(*results)


def write_out(*refs):
    sources, targets, sem = refs[:4], refs[4:8], refs[8]
    copies = [pltpu.make_async_copy(a, b, sem.at[i]) for i, (a, b) in enumerate(zip(sources, targets))]
    for copy in copies[::-1]:
        copy.start()
    for copy in copies:
        copy.wait()


def solution(mesh):
    ny, nz = mesh.shape["row"] // 2, mesh.shape["col"] // NX
    in_specs = (P("col", "row"), P("row", "col"), P("col", "row"), P("col", "row"))
    out_specs = (P("col", "row"), P("col", "row"), P("row", "col"), P("col", "row"))
    return jax.shard_map(
        functools.partial(local, ny, nz), mesh=mesh, in_specs=in_specs, out_specs=out_specs, check_vma=False
    )
```
